512 devices in a mesh: dp: 16 (over z, core), ctx: 32 (over x, y).
Axes of the slice: x: 4, y: 8, z: 8, core: 2. Of those that a mesh axis runs over, the one named last changes fastest.
Arguments:
- query_rows: bfloat16 [131072, 2048], P(('dp', 'ctx')), parts along dimension 0, may hold values from -64 to 64
- key_rows: bfloat16 [131072, 512], P(('dp', 'ctx')), parts along dimension 0, may hold values from -32 to 32
- value_rows: bfloat16 [131072, 512], P(('dp', 'ctx')), parts along dimension 0, may hold values from -6 to 6
- doc_lengths: int32 [288], P('dp'), parts along dimension 0, may hold values from 1 to 1793, 8192 in all
- row_owner: int32 [131072, 1], P(('dp', 'ctx')), parts along dimension 0, may hold values from 0 to 31; in each aligned block of 256 rows (0 to 255, 256 to 511, ...) at most 16 rows name the same one
Outputs:
- shard_rows: bfloat16 [262144, 2048], P(('dp', 'ctx')), parts along dimension 0
The draws below stay inside these ranges and needn't reach their ends.
There are 16 independent parts, one for each index of `dp`. The reference program is written for one: setup_inputs(seed, part) draws one part's arguments, and reference() takes and returns one part's arrays. A program takes and returns all parts, laid end to end along the dimension named above; each array names one. Nothing has to cross between parts.
Inputs may be any that keep to these rules, and one draw needn't show every extreme that they name: `doc_lengths`: the lengths sum to 8192; the largest is 1793. `row_owner`: among the rows of one shard at most 16 name the same owner, and in every draw some shard's rows name one owner exactly 16 times.
All inputs are finite; a program needn't handle non-finite values.
Results may differ from the reference program's by a relative error of at most 0.0036.
Values may be sent and summed in bfloat16 or wider, within the bound.
No kernel may reach another device: no remote copies, remote signals or barrier semaphores. Data moves between devices by JAX's collectives and lax.ppermute only.
A program may use at most 64 MiB of HBM per device.

```python
import math
import jax
import jax.numpy as jnp
import numpy as np
from jax import lax

H = 16
KVH = 4
HD = 128
TOK_DEV = 256
SPAN = 8
TOKENS = 8192
MAXDOC = 1793
NDOC = 18
PAIR = 16
RECV = 512
N_CTX = 32


def draw_key_rows(key, part):
    key = jax.random.fold_in(key, 1)
    drawn = jnp.clip(jax.random.normal(key, (TOKENS, KVH * HD), jnp.float32), -6.0, 6.0)
    return drawn.astype(jnp.bfloat16)


def draw_query_rows(key, part):
    key = jax.random.fold_in(key, 2)
    drawn = jnp.clip(jax.random.normal(key, (TOKENS, H * HD), jnp.float32), -6.0, 6.0)
    return drawn.astype(jnp.bfloat16)


def steps_of(stream_key, extent, split, low, top_value):
    factor_of = 1.0
    for position, blocks in split:
        heights = jax.random.uniform(jax.random.fold_in(jax.random.fold_in(stream_key, 6), position), (blocks,), jnp.float32, low / len(split), top_value / len(split))
        factor_of = factor_of * jnp.repeat(jnp.exp(heights), extent[position] // blocks).reshape((-1,) + (1,) * (len(extent) - 1 - position))
    return factor_of


def split_up(count, total, bound, skew):
    loads = [(1 << 20) // math.isqrt(grade ** skew) + 1 for grade in range(2, count + 1)]
    rest, counts = total - bound - (count - 1), [1] * (count - 1)
    while rest > 0:
        movable = [i for i in range(count - 1) if counts[i] < bound]
        mass, remaining = sum([loads[i] for i in movable]), rest
        for i in movable:
            addition = min(bound - counts[i], max(1, remaining * loads[i] // mass), rest)
            counts[i] = counts[i] + addition
            rest = rest - addition
    return np.array([bound] + counts)


def ragged_sizes(stream_key, amount, total, limit, slope):
    if amount == 2:
        one = jax.random.randint(stream_key, (), max(1, total - limit), min(limit, total - 1) + 1)
        return jnp.stack([one, total - one])
    tallies = jnp.asarray(split_up(amount, total, limit, slope), jnp.int32)
    pairs = (amount - 1) // 2
    giver, taker = tallies[1:1 + 2 * pairs:2], tallies[2:2 + 2 * pairs:2]
    slack = jnp.minimum(giver - 1, limit - taker)
    shifted = jax.random.randint(jax.random.fold_in(stream_key, 1), (pairs,), 0, 1 << 20) % (slack + 1)
    tallies = tallies.at[1:1 + 2 * pairs:2].set(giver - shifted).at[2:2 + 2 * pairs:2].set(taker + shifted)
    return tallies[jax.random.permutation(jax.random.fold_in(stream_key, 2), amount)]


def assign_block(rng, own, number, rows, amount, top, reach, skew):
    ranking = jax.random.permutation(rng, amount)
    heavy_load, ordinary = shares(amount, rows * top, reach, skew, True), shares(amount, rows * top, reach, skew, False)
    places = jnp.arange(amount)

    def named(tallies, rotation):
        used = int((tallies > 0).sum())
        fixed = max(1, used // 4)
        shifted = fixed + (places - fixed + rotation * (used - fixed)) % max(1, amount - fixed)
        return jnp.zeros((amount,), jnp.int32).at[ranking[jnp.where(places < fixed, places, shifted)]].set(jnp.asarray(tallies, jnp.int32))

    tallies = jnp.where(number % 4 == 0, named(heavy_load, number // 4), named(ordinary, number - number // 4 - 1))
    mixed = jax.random.permutation(jax.random.fold_in(own, 3), amount)
    source_of, sink = mixed[0:amount // 2 * 2:2], mixed[1:amount // 2 * 2:2]
    margin = jnp.minimum(tallies[source_of] - 1, reach - tallies[sink]) // 2
    margin = jnp.where((source_of == ranking[0]) | (sink == ranking[0]) | (tallies[sink] == 0), 0, jnp.maximum(margin, 0))
    shifted = jax.random.randint(jax.random.fold_in(own, 4), (amount // 2,), 0, 1 << 20) % (margin + 1)
    tallies = tallies.at[source_of].add(-shifted).at[sink].add(shifted)
    items = jnp.searchsorted(jnp.cumsum(tallies), jnp.arange(rows * top), side="right").astype(jnp.int32)
    grid = items.reshape(top, rows).T
    grid = grid[jax.random.permutation(jax.random.fold_in(own, 1), rows)]
    rotation = jax.random.randint(jax.random.fold_in(own, 2), (rows, 1), 0, top)
    return jnp.take_along_axis(grid, (jnp.arange(top)[None, :] + rotation) % top, axis=1)


def shares(count, total, most, slope, full):
    loads = [(1 << 20) // math.isqrt(rank ** slope) + 1 for rank in range(1, count + 1)]
    largest = most if full else min(most, max(-(-total // count), total * loads[0] // sum(loads)))
    least = 1 if total - largest >= count - 1 else 0
    holding, spare = [largest] + [least] * (count - 1), total - largest - least * (count - 1)
    while spare > 0:
        movable = [i for i in range(1, count) if holding[i] < largest] or [i for i in range(1, count) if holding[i] < most]
        pool, remaining = sum([loads[i] for i in movable]), spare
        for i in movable:
            extra = min(most - holding[i], max(1, remaining * loads[i] // pool), spare)
            holding[i] = holding[i] + extra
            spare = spare - extra
    return np.array(holding)


def bell_draw(own_key, shape, deviation, reach, pieces=(), kind=jnp.bfloat16):
    drawn = jax.random.normal(own_key, shape, jnp.float32) * deviation
    if len(pieces) > 0:
        drawn = steps_of(own_key, shape, pieces, -0.22, 0.18) * drawn
    return jnp.clip(drawn, min=-reach, max=reach).astype(kind)


def setup_inputs(seed: int = 0, part: int = 0) -> dict:
    arg_keys = jax.random.split(jax.random.key(seed), 6)
    own_keys = jax.random.split(jax.random.fold_in(arg_keys[5], part), 6)
    query_rows = draw_query_rows(jax.random.fold_in(jax.random.fold_in(arg_keys[5], part), 71), part)
    key_rows = draw_key_rows(jax.random.fold_in(jax.random.fold_in(arg_keys[5], part), 71), part)
    value_rows = bell_draw(own_keys[2], (TOKENS, KVH * HD), 1.0, 6.0, ((0, 32),))
    doc_lengths = ragged_sizes(own_keys[3], NDOC, TOKENS, MAXDOC, 1).astype(jnp.int32)
    row_owner_keys = jax.random.split(jax.random.fold_in(own_keys[4], 1), TOKENS // TOK_DEV)
    row_owner_turns = jax.random.permutation(jax.random.fold_in(own_keys[4], 3), TOKENS // TOK_DEV)
    row_owner = jax.vmap(lambda own, number: assign_block(jax.random.fold_in(own_keys[4], 2), own, number, TOK_DEV, N_CTX, 1, PAIR, 2))(row_owner_keys, row_owner_turns).reshape((TOKENS, 1))
    return dict(query_rows=query_rows, key_rows=key_rows, value_rows=value_rows, doc_lengths=doc_lengths, row_owner=row_owner)


def segment_of(positions, doc_lengths):
    doc_ends = jnp.cumsum(doc_lengths).astype(jnp.int32)
    return lax.optimization_barrier(jnp.sum((doc_ends[None, :] <= positions[:, None]).astype(jnp.int32), axis=1))

def window_attention(query_block, key_window, value_window, query_pos, key_pos, doc_lengths):
    row_count = query_block.shape[0]
    span_rows = key_window.shape[0]
    group_size = H // KVH
    query_seg = segment_of(query_pos, doc_lengths)
    key_seg = segment_of(key_pos, doc_lengths)
    visible = (query_seg[:, None] == key_seg[None, :]) & (key_pos[None, :] <= query_pos[:, None]) & (key_pos[None, :] >= 0)
    queries = query_block.reshape(row_count, KVH, group_size, HD).astype(jnp.float32)
    keyed = key_window.reshape(span_rows, KVH, HD).astype(jnp.float32)
    valued = value_window.reshape(span_rows, KVH, HD).astype(jnp.float32)
    scores = jnp.einsum('qkgd,nkd->qkgn', queries, keyed) * (1.0 / math.sqrt(HD))
    mask = visible[:, None, None, :]
    scores = jnp.where(mask, scores, -jnp.inf)
    row_max = lax.optimization_barrier(jnp.max(scores, axis=3, keepdims=True))
    expo = jnp.where(mask, jnp.exp(scores - row_max), 0.0)
    denominator = lax.optimization_barrier(jnp.sum(expo, axis=3))
    weights = expo.astype(jnp.bfloat16)
    weighted = jnp.einsum('qkgn,nkd->qkgd', weights.astype(jnp.float32), valued)
    attended = weighted / denominator[..., None]
    return attended.reshape(row_count, H * HD).astype(jnp.bfloat16)

def reference(query_rows, key_rows, value_rows, doc_lengths, row_owner):
    row_count = TOK_DEV
    back_rows = (SPAN - 1) * row_count
    padded_keys = jnp.concatenate([jnp.zeros((back_rows, key_rows.shape[1]), key_rows.dtype), key_rows], axis=0)
    padded_values = jnp.concatenate([jnp.zeros((back_rows, value_rows.shape[1]), value_rows.dtype), value_rows], axis=0)

    def shard_output(shard_index):
        start = (shard_index * row_count).astype(jnp.int32)
        query_block = lax.dynamic_slice_in_dim(query_rows, start, row_count, 0)
        key_window = lax.dynamic_slice_in_dim(padded_keys, start, SPAN * row_count, 0)
        value_window = lax.dynamic_slice_in_dim(padded_values, start, SPAN * row_count, 0)
        query_pos = start + jnp.arange(row_count, dtype=jnp.int32)
        key_pos = start - back_rows + jnp.arange(SPAN * row_count, dtype=jnp.int32)
        return window_attention(query_block, key_window, value_window, query_pos, key_pos, doc_lengths)
    blocks = lax.map(shard_output, jnp.arange(N_CTX, dtype=jnp.int32))
    sequence_out = blocks.reshape(TOKENS, H * HD)
    owners = row_owner[:, 0].reshape(N_CTX, row_count)
    onehot = (owners[:, :, None] == jnp.arange(N_CTX, dtype=jnp.int32)[None, None, :]).astype(jnp.int32)
    running = jnp.cumsum(onehot, axis=1)
    slot_rank = lax.optimization_barrier(jnp.sum(onehot * (running - 1), axis=2))
    sources = jnp.arange(N_CTX, dtype=jnp.int32)[:, None]
    target = (owners * RECV + sources * PAIR + slot_rank).reshape(TOKENS).astype(jnp.int32)
    shard_rows = jnp.zeros((N_CTX * RECV, H * HD), jnp.bfloat16).at[target].set(sequence_out)
    return shard_rows
```

```python
import functools
import math

import jax
import jax.numpy as jnp
from jax import lax
from jax.experimental import pallas as pl
from jax.experimental.pallas import tpu as pltpu
from jax.sharding import PartitionSpec as P

H = 16
KVH = 4
HD = 128
GROUP = H // KVH
SPAN = 8
SCALE = math.log2(math.e) / math.sqrt(HD)


def shift(value, steps):
    count = lax.axis_size("ctx")
    return lax.ppermute(value, "ctx", [(s, (s + steps) % count) for s in range(count)])


def doc_starts(doc_ref, positions):
    end = jnp.int32(0)
    starts = jnp.zeros_like(positions)
    for k in range(doc_ref.shape[0]):
        end = end + doc_ref[k]
        starts = jnp.where(end <= positions, end, starts)
    return starts


def attend(first, last, dists, *refs):
    refs = list(refs)
    index_ref, doc_ref, q_ref = refs[:3]
    refs = refs[3:]
    pairs = [(d, refs.pop(0), refs.pop(0)) for d in dists]
    rows = q_ref.shape[0]
    base = index_ref[0] * rows
    if not first:
        m_in, l_in, acc_in = refs[:3]
        refs = refs[3:]
    if last:
        owner_col, owner_row, out_ref, m_ref, l_ref, acc_ref, hot_ref = refs
    else:
        m_ref, l_ref, acc_ref = refs
    positions = base + lax.broadcasted_iota(jnp.int32, (1, rows), 1)
    starts = doc_starts(doc_ref, positions)
    earliest = doc_starts(doc_ref, base)
    key_row = lax.broadcasted_iota(jnp.int32, (rows, rows), 0)

    if not first:
        m_ref[...] = m_in[...]
        l_ref[...] = l_in[...]
        acc_ref[...] = acc_in[...]

    def visit(d, k_ref, v_ref):
        key_pos = base - d * rows + key_row
        visible = key_pos >= starts
        if d == 0:
            visible = visible & (key_pos <= positions)
        k, v = k_ref[...], v_ref[...]
        for g in range(GROUP):
            q = q_ref[:, g * HD : (g + 1) * HD]
            scores = lax.dot_general(
                k, q, (((1,), (1,)), ((), ())), preferred_element_type=jnp.float32
            )
            scores = jnp.where(visible, scores, -jnp.inf)
            top = jnp.max(scores, axis=0, keepdims=True)
            if d > 0:
                before = m_ref[0, g : g + 1, :]
                top = jnp.maximum(before, top)
            expo = jnp.exp2((scores - top) * SCALE)
            total = jnp.sum(expo, axis=0, keepdims=True)
            weighted = lax.dot_general(
                v, expo.astype(jnp.bfloat16), (((0,), (0,)), ((), ())), preferred_element_type=jnp.float32
            )
            if d > 0:
                keep = jnp.exp2((before - top) * SCALE)
                total = l_ref[0, g : g + 1, :] * keep + total
                weighted = acc_ref[0, g * HD : (g + 1) * HD, :] * keep + weighted
            m_ref[0, g : g + 1, :] = top
            l_ref[0, g : g + 1, :] = total
            acc_ref[0, g * HD : (g + 1) * HD, :] = weighted

    for d, k_ref, v_ref in pairs:
        if d == 0:
            visit(d, k_ref, v_ref)
        else:
            pl.when(earliest < base - (d - 1) * rows)(functools.partial(visit, d, k_ref, v_ref))

    if last:
        slots = out_ref.shape[0]

        @pl.when(pl.program_id(0) == 0)
        def _():
            same = (owner_col[...] == owner_row[...]) & (
                key_row < lax.broadcasted_iota(jnp.int32, (rows, rows), 1)
            )
            rank = jnp.sum(same.astype(jnp.int32), axis=0, keepdims=True)
            slot = owner_row[...] * (slots // 32) + rank
            spots = lax.broadcasted_iota(jnp.int32, (slots, rows), 0)
            hot_ref[...] = (spots == slot).astype(jnp.bfloat16)

        for g in range(GROUP):
            attended = acc_ref[0, g * HD : (g + 1) * HD, :] / l_ref[0, g : g + 1, :]
            out_ref[:, g * HD : (g + 1) * HD] = lax.dot_general(
                hot_ref[...], attended.astype(jnp.bfloat16), (((1,), (1,)), ((), ())),
                preferred_element_type=jnp.float32,
            ).astype(jnp.bfloat16)


def step(index, doc_lengths, query_rows, blocks, state=None, owners=None):
    rows, features = query_rows.shape
    first, last = state is None, owners is not None
    dists = [d for d, _, _ in blocks]
    smem = pl.BlockSpec(memory_space=pltpu.SMEM)
    by_head = lambda width: pl.BlockSpec((rows, width), lambda h: (0, h))
    stat = pl.BlockSpec((1, GROUP, rows), lambda h: (h, 0, 0))
    sums = pl.BlockSpec((1, GROUP * HD, rows), lambda h: (h, 0, 0))
    operands, in_specs = [index, doc_lengths, query_rows], [smem, smem, by_head(GROUP * HD)]
    for _, k, v in blocks:
        operands += [k, v]
        in_specs += [by_head(HD), by_head(HD)]
    if not first:
        operands += list(state)
        in_specs += [stat, stat, sums]
    if last:
        slots = 2 * rows
        operands += [owners, owners.reshape(1, rows)]
        in_specs += [pl.BlockSpec((rows, 1), lambda h: (0, 0)), pl.BlockSpec((1, rows), lambda h: (0, 0))]
        out_shape = jax.ShapeDtypeStruct((slots, features), jnp.bfloat16)
        out_specs = pl.BlockSpec((slots, GROUP * HD), lambda h: (0, h))
        scratch = [
            pltpu.VMEM((1, GROUP, rows), jnp.float32),
            pltpu.VMEM((1, GROUP, rows), jnp.float32),
            pltpu.VMEM((1, GROUP * HD, rows), jnp.float32),
            pltpu.VMEM((slots, rows), jnp.bfloat16),
        ]
    else:
        out_shape = [
            jax.ShapeDtypeStruct((KVH, GROUP, rows), jnp.float32),
            jax.ShapeDtypeStruct((KVH, GROUP, rows), jnp.float32),
            jax.ShapeDtypeStruct((KVH, GROUP * HD, rows), jnp.float32),
        ]
        out_specs = [stat, stat, sums]
        scratch = []
    flops = len(dists) * 4 * rows * rows * features
    return pl.pallas_call(
        functools.partial(attend, first, last, dists),
        grid=(KVH,),
        in_specs=in_specs,
        out_specs=out_specs,
        out_shape=out_shape,
        scratch_shapes=scratch,
        compiler_params=pltpu.CompilerParams(vmem_limit_bytes=32 << 20),
        cost_estimate=pl.CostEstimate(
            flops=flops, bytes_accessed=6 << 20, transcendentals=len(dists) * rows * rows * H
        ),
    )(*operands)


def on_device(query_rows, key_rows, value_rows, doc_lengths, row_owner):
    rows, features = query_rows.shape
    devices = lax.axis_size("ctx")
    index = lax.axis_index("ctx").astype(jnp.int32).reshape(1)
    near, far = {0: (key_rows, value_rows)}, {8: (key_rows, value_rows)}
    for hop in range(1, 4):
        near[hop] = tuple(shift(x, 1) for x in near[hop - 1])
        far[8 - hop] = tuple(shift(x, SPAN - 1 if hop == 1 else -1) for x in far[9 - hop])
    middle = (shift(near[3][0], 1), shift(far[5][1], -1))

    state = step(index, doc_lengths, query_rows, [(0, key_rows, value_rows)])
    for hop in range(1, 4):
        state = step(
            index, doc_lengths, query_rows, [(hop, *near[hop]), (8 - hop, *far[8 - hop])], state
        )
    outgoing = step(index, doc_lengths, query_rows, [(4, *middle)], state, row_owner)
    received = lax.all_to_all(
        outgoing.reshape(devices, -1, features), "ctx", split_axis=0, concat_axis=0, tiled=True
    )
    return received.reshape(-1, features)


def solution(mesh):
    rows = P(("dp", "ctx"), None)
    return jax.shard_map(
        on_device,
        mesh=mesh,
        in_specs=(rows, rows, rows, P("dp"), rows),
        out_specs=rows,
        check_vma=False,
    )
```

```python
import functools
import math

import jax
import jax.numpy as jnp
from jax import lax
from jax.experimental import pallas as pl
from jax.experimental.pallas import tpu as pltpu
from jax.sharding import PartitionSpec as P

H = 16
KVH = 4
HD = 128
GROUP = H // KVH
SPAN = 8
SCALE = math.log2(math.e) / math.sqrt(HD)


def shift(value, steps):
    count = lax.axis_size("ctx")
    return lax.ppermute(value, "ctx", [(s, (s + steps) % count) for s in range(count)])


def doc_start(doc_ref, positions):
    end = jnp.int32(0)
    start = jnp.zeros_like(positions)
    for k in range(doc_ref.shape[0]):
        end = end + doc_ref[k]
        start = jnp.where(end <= positions, end, start)
    return start


def over_group(row):
    return jnp.concatenate([row] * GROUP, axis=1)


def visit(d, base, starts, positions, q_ref, k_ref, v_ref, m_ref, l_ref, acc_ref):
    rows = k_ref.shape[0]
    key_pos = base - d * rows + lax.broadcasted_iota(jnp.int32, (rows, rows), 0)
    visible = key_pos >= starts
    if d == 0:
        visible = visible & (key_pos <= positions)
    scores = lax.dot_general(
        k_ref[...], q_ref[0], (((1,), (0,)), ((), ())), preferred_element_type=jnp.float32
    )
    scores = jnp.where(over_group(visible), scores, -jnp.inf)
    top = jnp.max(scores, axis=0, keepdims=True)
    if d > 0:
        before = m_ref[0]
        top = jnp.maximum(before, top)
    expo = jnp.exp2((scores - top) * SCALE)
    total = jnp.sum(expo, axis=0, keepdims=True)
    weighted = lax.dot_general(
        v_ref[...], expo.astype(jnp.bfloat16), (((0,), (0,)), ((), ())), preferred_element_type=jnp.float32
    )
    if d > 0:
        keep = jnp.exp2((before - top) * SCALE)
        total = l_ref[0] * keep + total
        weighted = acc_ref[0] * keep + weighted
    m_ref[0] = top
    l_ref[0] = total
    acc_ref[0] = weighted


def begin(devices, index_ref, doc_ref, q_ref, k_ref, v_ref, col_ref, row_ref, m_ref, l_ref, acc_ref, hot_ref):
    rows, slots = k_ref.shape[0], hot_ref.shape[0]
    base = index_ref[0] * rows
    positions = base + lax.broadcasted_iota(jnp.int32, (1, rows), 1)
    starts = doc_start(doc_ref, positions)
    visit(0, base, starts, positions, q_ref, k_ref, v_ref, m_ref, l_ref, acc_ref)

    @pl.when(pl.program_id(0) == 0)
    def _():
        earlier = lax.broadcasted_iota(jnp.int32, (rows, rows), 0) < lax.broadcasted_iota(
            jnp.int32, (rows, rows), 1
        )
        same = (col_ref[...] == row_ref[...]) & earlier
        rank = jnp.sum(same.astype(jnp.int32), axis=0, keepdims=True)
        slot = row_ref[...] * (slots // devices) + rank
        spots = lax.broadcasted_iota(jnp.int32, (slots, rows), 0)
        hot_ref[...] = (spots == slot).astype(jnp.float32).astype(jnp.bfloat16)


def proceed(dists, last, index_ref, doc_ref, q_ref, *refs):
    refs = list(refs)
    blocks = [(d, refs.pop(0), refs.pop(0)) for d in dists]
    m_in, l_in, acc_in = refs[:3]
    if last:
        hot_ref, out_ref, m_ref, l_ref, acc_ref = refs[3:]
    else:
        m_ref, l_ref, acc_ref = refs[3:]
    rows = q_ref.shape[2] // GROUP
    base = index_ref[0] * rows
    earliest = doc_start(doc_ref, base)
    m_ref[...] = m_in[...]
    l_ref[...] = l_in[...]
    acc_ref[...] = acc_in[...]

    for d, k_ref, v_ref in blocks:

        @pl.when(earliest < base - (d - 1) * rows)
        def _(d=d, k_ref=k_ref, v_ref=v_ref):
            positions = base + lax.broadcasted_iota(jnp.int32, (1, rows), 1)
            starts = doc_start(doc_ref, positions)
            visit(d, base, starts, positions, q_ref, k_ref, v_ref, m_ref, l_ref, acc_ref)

    if last:
        attended = (acc_ref[0] / l_ref[0]).astype(jnp.bfloat16)
        for g in range(GROUP):
            out_ref[:, g * HD : (g + 1) * HD] = lax.dot_general(
                hot_ref[...], attended[:, g * rows : (g + 1) * rows], (((1,), (1,)), ((), ())),
                preferred_element_type=jnp.float32,
            ).astype(jnp.bfloat16)


SMEM = pl.BlockSpec(memory_space=pltpu.SMEM)


def whole(shape):
    return pl.BlockSpec(shape, lambda h: (0,) * len(shape))


def per_head(*shape):
    return pl.BlockSpec((1, *shape), lambda h: (h, 0, 0))


def block_specs(rows):
    return [pl.BlockSpec((rows, HD), lambda h: (0, h)), pl.BlockSpec((rows, HD), lambda h: (1, h))]


def running(rows):
    sizes = [(1, GROUP * rows), (1, GROUP * rows), (HD, GROUP * rows)]
    return [jax.ShapeDtypeStruct((KVH, *s), jnp.float32) for s in sizes], [per_head(*s) for s in sizes]


def cost(rows, blocks):
    return pl.CostEstimate(
        flops=blocks * 4 * rows * rows * H * HD, bytes_accessed=6 << 20, transcendentals=blocks * rows * rows * H
    )


PARAMS = pltpu.CompilerParams(vmem_limit_bytes=32 << 20)


def first_step(index, doc_lengths, queries, block, row_owner, devices):
    rows = block.shape[0] // 2
    shapes, specs = running(rows)
    return pl.pallas_call(
        functools.partial(begin, devices),
        grid=(KVH,),
        in_specs=[SMEM, SMEM, per_head(HD, GROUP * rows), *block_specs(rows), whole((rows, 1)), whole((1, rows))],
        out_specs=[*specs, whole((2 * rows, rows))],
        out_shape=[*shapes, jax.ShapeDtypeStruct((2 * rows, rows), jnp.bfloat16)],
        compiler_params=PARAMS,
        cost_estimate=cost(rows, 1),
    )(index, doc_lengths, queries, block, block, row_owner, row_owner.reshape(1, rows))


def next_step(index, doc_lengths, queries, blocks, state):
    rows = blocks[0][1].shape[0] // 2
    shapes, specs = running(rows)
    return pl.pallas_call(
        functools.partial(proceed, [d for d, _ in blocks], False),
        grid=(KVH,),
        in_specs=[SMEM, SMEM, per_head(HD, GROUP * rows), *block_specs(rows) * len(blocks), *specs],
        out_specs=specs,
        out_shape=shapes,
        compiler_params=PARAMS,
        cost_estimate=cost(rows, len(blocks)),
    )(index, doc_lengths, queries, *[b for _, block in blocks for b in (block, block)], *state)


def last_step(index, doc_lengths, queries, keys, values, state, hot):
    rows = hot.shape[1]
    _, specs = running(rows)
    flat = pl.BlockSpec((rows, HD), lambda h: (0, h))
    return pl.pallas_call(
        functools.partial(proceed, [SPAN // 2], True),
        grid=(KVH,),
        in_specs=[SMEM, SMEM, per_head(HD, GROUP * rows), flat, flat, *specs, whole(hot.shape)],
        out_specs=pl.BlockSpec((hot.shape[0], GROUP * HD), lambda h: (0, h)),
        out_shape=jax.ShapeDtypeStruct((hot.shape[0], H * HD), jnp.bfloat16),
        scratch_shapes=[pltpu.VMEM(s.block_shape, jnp.float32) for s in specs],
        compiler_params=PARAMS,
        cost_estimate=cost(rows, 1),
    )(index, doc_lengths, queries, keys, values, *state, hot)


def on_device(query_rows, key_rows, value_rows, doc_lengths, row_owner):
    rows, features = query_rows.shape
    devices = lax.axis_size("ctx")
    index = lax.axis_index("ctx").astype(jnp.int32).reshape(1)
    block = jnp.concatenate([key_rows, value_rows], axis=0)
    near, far = shift(block, 1), shift(block, SPAN - 1)
    queries = query_rows.reshape(rows, KVH, GROUP, HD).transpose(1, 3, 2, 0).reshape(KVH, HD, GROUP * rows)
    *state, hot = first_step(index, doc_lengths, queries, block, row_owner, devices)
    for d in range(1, SPAN // 2):
        near, far, *state = lax.optimization_barrier((near, far, *state))
        if d + 1 < SPAN // 2:
            coming = shift(near, 1), shift(far, -1)
        else:
            coming = shift(near[:rows], 1), shift(far[rows:], -1)
        state = next_step(index, doc_lengths, queries, [(d, near), (SPAN - d, far)], state)
        near, far = coming
    outgoing = last_step(index, doc_lengths, queries, near, far, state, hot)
    received = lax.all_to_all(
        outgoing.reshape(devices, -1, features), "ctx", split_axis=0, concat_axis=0, tiled=True
    )
    return received.reshape(-1, features)


def solution(mesh):
    rows = P(("dp", "ctx"), None)
    return jax.shard_map(
        on_device,
        mesh=mesh,
        in_specs=(rows, rows, rows, P("dp"), rows),
        out_specs=rows,
        check_vma=False,
    )
```

```python
import functools
import math

import jax
import jax.numpy as jnp
from jax import lax
from jax.experimental import pallas as pl
from jax.experimental.pallas import tpu as pltpu
from jax.sharding import PartitionSpec as P

H = 16
KVH = 4
HD = 128
GROUP = H // KVH
TEAM = 4
PAD = 16
SCALE = math.log2(math.e) / math.sqrt(HD)
NT = (((1,), (1,)), ((), ()))
SMEM = pl.BlockSpec(memory_space=pltpu.SMEM)
VMEM = pl.BlockSpec(memory_space=pltpu.VMEM)


def doc_start(doc_ref, positions):
    end = jnp.int32(0)
    start = jnp.zeros_like(positions)
    for k in range(doc_ref.shape[0]):
        end = end + doc_ref[k]
        start = jnp.where(end <= positions, end, start)
    return start


def split(index_ref, q_ref, k_ref, v_ref, owner_ref, kv_out, q_out):
    rows = k_ref.shape[0]
    odd = lax.rem(lax.div(index_ref[0], TEAM), 2) == 1
    owners = jnp.broadcast_to(owner_ref[...], (PAD, rows)).astype(jnp.float32).astype(jnp.bfloat16)
    for h in range(KVH):
        member = jnp.where(odd, KVH - 1 - h, h)
        head = slice(h * HD, (h + 1) * HD)
        kv_out[member, :rows, :HD] = k_ref[:, head]
        kv_out[member, :rows, HD:] = v_ref[:, head]
        kv_out[member, rows:, :] = owners
        q_out[member] = q_ref[:, h * GROUP * HD : (h + 1) * GROUP * HD]


def over_group(row):
    return jnp.concatenate([row] * GROUP, axis=1)


def attend(devices, index_ref, doc_ref, q_ref, own_ref, back_ref, far_ref, out_ref, q_t, m_ref, l_ref, acc_ref):
    i = pl.program_id(0)
    rows = q_ref.shape[1]
    first_shard = lax.div(index_ref[0], TEAM) * TEAM
    base = (first_shard + i) * rows
    positions = base + lax.broadcasted_iota(jnp.int32, (1, rows), 1)
    starts = doc_start(doc_ref, positions)
    turned = q_ref[0].T
    q_t[...] = jnp.concatenate([turned[g * HD : (g + 1) * HD] for g in range(GROUP)], axis=1)

    def visit(block_ref, place, shard, first):
        k, v = block_ref[place, :rows, :HD], block_ref[place, :rows, HD:]
        key_pos = (first_shard + shard) * rows + lax.broadcasted_iota(jnp.int32, (rows, rows), 0)
        visible = key_pos >= starts
        if first:
            visible = visible & (key_pos <= positions)
        scores = jnp.dot(k, q_t[...], preferred_element_type=jnp.float32)
        scores = jnp.where(over_group(visible), scores, -jnp.inf)
        top = jnp.max(scores, axis=0, keepdims=True)
        if not first:
            before = m_ref[...]
            top = jnp.maximum(before, top)
        expo = jnp.exp2((scores - top) * SCALE)
        total = jnp.sum(expo, axis=0, keepdims=True)
        weighted = lax.dot_general(
            v, expo.astype(jnp.bfloat16), (((0,), (0,)), ((), ())), preferred_element_type=jnp.float32
        )
        if not first:
            keep = jnp.exp2((before - top) * SCALE)
            total = l_ref[...] * keep + total
            weighted = acc_ref[...] * keep + weighted
        m_ref[...] = top
        l_ref[...] = total
        acc_ref[...] = weighted

    visit(own_ref, i, i, True)
    lowest = jnp.maximum(lax.div(doc_start(doc_ref, base), rows) - first_shard, i - 7)
    for ref, low in ((own_ref, 0), (back_ref, -TEAM), (far_ref, -2 * TEAM)):

        @pl.loop(jnp.maximum(lowest, low), jnp.minimum(i, low + TEAM))
        def _(shard, ref=ref, low=low):
            visit(ref, shard - low, shard, False)

    owner_row = own_ref[i, rows : rows + PAD, :][:1].astype(jnp.float32)
    across = jnp.broadcast_to(owner_row, (rows, rows))
    earlier = lax.broadcasted_iota(jnp.int32, (rows, rows), 0) < lax.broadcasted_iota(jnp.int32, (rows, rows), 1)
    same = (across == across.T) & earlier
    rank = jnp.sum(same.astype(jnp.int32), axis=0, keepdims=True)
    slots = 2 * rows
    slot = owner_row.astype(jnp.int32) * (slots // devices) + rank
    spots = lax.broadcasted_iota(jnp.int32, (slots, rows), 0)
    hot = (spots == slot).astype(jnp.float32).astype(jnp.bfloat16)
    attended = (acc_ref[...] / l_ref[...]).astype(jnp.bfloat16)
    attended = jnp.concatenate([attended[:, g * rows : (g + 1) * rows] for g in range(GROUP)], axis=0)
    placed = lax.dot_general(hot, attended, NT, preferred_element_type=jnp.float32).astype(jnp.bfloat16)
    out_ref[:, 0] = placed.reshape(devices, slots // devices, GROUP * HD)


def gather_heads(in_ref, out_ref):
    depth, width = in_ref.shape[1:]
    for team in range(2):
        for member in range(TEAM):
            h = KVH - 1 - member if team else member
            out_ref[team * depth : (team + 1) * depth, h * width : (h + 1) * width] = in_ref[team * TEAM + member]


def on_device(query_rows, key_rows, value_rows, doc_lengths, row_owner):
    rows, features = query_rows.shape
    devices = lax.axis_size("ctx")
    teams = devices // TEAM
    index = lax.axis_index("ctx").astype(jnp.int32).reshape(1)
    params = pltpu.CompilerParams(vmem_limit_bytes=40 << 20)
    groups = [[t * TEAM + m for m in range(TEAM)] for t in range(teams)]
    width = GROUP * HD

    kv, queries = pl.pallas_call(
        split,
        in_specs=[SMEM] + [VMEM] * 4,
        out_specs=[VMEM] * 2,
        out_shape=[
            jax.ShapeDtypeStruct((TEAM, rows + PAD, 2 * HD), jnp.bfloat16),
            jax.ShapeDtypeStruct((TEAM, rows, width), jnp.bfloat16),
        ],
        compiler_params=params,
    )(index, query_rows, key_rows, value_rows, row_owner.reshape(1, rows))
    own = lax.all_to_all(kv, "ctx", 0, 0, axis_index_groups=groups, tiled=True)
    own, queries = lax.optimization_barrier((own, queries))
    back = lax.ppermute(
        own, "ctx",
        [(t * TEAM + m, (t + 1) * TEAM + TEAM - 1 - m) for t in range(teams - 1) for m in range(TEAM)],
    )
    far = lax.ppermute(own, "ctx", [(s, s + 2 * TEAM) for s in range(devices - 2 * TEAM)])
    queries = lax.all_to_all(queries, "ctx", 0, 0, axis_index_groups=groups, tiled=True)

    slots = 2 * rows // devices
    outgoing = pl.pallas_call(
        functools.partial(attend, devices),
        grid=(TEAM,),
        in_specs=[SMEM, SMEM, pl.BlockSpec((1, rows, width), lambda i: (i, 0, 0)), VMEM, VMEM, VMEM],
        out_specs=pl.BlockSpec((devices, 1, slots, width), lambda i: (0, i, 0, 0)),
        out_shape=jax.ShapeDtypeStruct((devices, TEAM, slots, width), jnp.bfloat16),
        scratch_shapes=[
            pltpu.VMEM((HD, GROUP * rows), jnp.bfloat16),
            pltpu.VMEM((1, GROUP * rows), jnp.float32),
            pltpu.VMEM((1, GROUP * rows), jnp.float32),
            pltpu.VMEM((HD, GROUP * rows), jnp.float32),
        ],
        compiler_params=params,
    )(index, doc_lengths, queries, own, back, far)
    received = lax.all_to_all(
        outgoing.reshape(devices, TEAM * slots, width), "ctx", split_axis=0, concat_axis=0, tiled=True
    )
    return pl.pallas_call(
        gather_heads,
        grid=(teams // 2,),
        in_specs=[pl.BlockSpec((2 * TEAM, TEAM * slots, width), lambda t: (t, 0, 0))],
        out_specs=pl.BlockSpec((2 * TEAM * slots, features), lambda t: (t, 0)),
        out_shape=jax.ShapeDtypeStruct((devices * slots, features), jnp.bfloat16),
        compiler_params=params,
    )(received)


def solution(mesh):
    rows = P(("dp", "ctx"), None)
    return jax.shard_map(
        on_device,
        mesh=mesh,
        in_specs=(rows, rows, rows, P("dp"), rows),
        out_specs=rows,
        check_vma=False,
    )
```

```python
import functools
import math

import jax
import jax.numpy as jnp
from jax import lax
from jax.experimental import pallas as pl
from jax.experimental.pallas import tpu as pltpu
from jax.sharding import PartitionSpec as P

H = 16
KVH = 4
HD = 128
GROUP = H // KVH
SPAN = 8
SCALE = math.log2(math.e) / math.sqrt(HD)


def shift(value, steps):
    count = lax.axis_size("ctx")
    return lax.ppermute(value, "ctx", [(s, (s + steps) % count) for s in range(count)])


def doc_start(doc_ref, positions):
    end = jnp.int32(0)
    start = jnp.zeros_like(positions)
    for k in range(doc_ref.shape[0]):
        end = end + doc_ref[k]
        start = jnp.where(end <= positions, end, start)
    return start


def over_group(row):
    return jnp.concatenate([row] * GROUP, axis=1)


def visit(d, base, starts, positions, q_ref, k_ref, v_ref, old, new):
    m_old, l_old, acc_old = old if d > 0 else (None, None, None)
    m_ref, l_ref, acc_ref = new
    rows = k_ref.shape[0]
    key_pos = base - d * rows + lax.broadcasted_iota(jnp.int32, (rows, rows), 0)
    visible = key_pos >= starts
    if d == 0:
        visible = visible & (key_pos <= positions)
    scores = lax.dot_general(
        k_ref[...], q_ref[0], (((1,), (0,)), ((), ())), preferred_element_type=jnp.float32
    )
    scores = jnp.where(over_group(visible), scores, -jnp.inf)
    top = jnp.max(scores, axis=0, keepdims=True)
    if d > 0:
        before = m_old[0]
        top = jnp.maximum(before, top)
    expo = jnp.exp2((scores - top) * SCALE)
    total = jnp.sum(expo, axis=0, keepdims=True)
    weighted = lax.dot_general(
        v_ref[...], expo.astype(jnp.bfloat16), (((0,), (0,)), ((), ())), preferred_element_type=jnp.float32
    )
    if d > 0:
        keep = jnp.exp2((before - top) * SCALE)
        total = l_old[0] * keep + total
        weighted = acc_old[0] * keep + weighted
    m_ref[0] = top
    l_ref[0] = total
    acc_ref[0] = weighted


def begin(devices, index_ref, doc_ref, rows_ref, k_ref, v_ref, col_ref, row_ref, m_ref, l_ref, acc_ref, q_ref, hot_ref):
    rows, slots = k_ref.shape[0], hot_ref.shape[0]
    turned = rows_ref[...].T
    q_ref[0] = jnp.concatenate([turned[g * HD : (g + 1) * HD] for g in range(GROUP)], axis=1)
    base = index_ref[0] * rows
    positions = base + lax.broadcasted_iota(jnp.int32, (1, rows), 1)
    starts = doc_start(doc_ref, positions)
    visit(0, base, starts, positions, q_ref, k_ref, v_ref, None, (m_ref, l_ref, acc_ref))

    @pl.when(pl.program_id(0) == 0)
    def _():
        earlier = lax.broadcasted_iota(jnp.int32, (rows, rows), 0) < lax.broadcasted_iota(
            jnp.int32, (rows, rows), 1
        )
        same = (col_ref[...] == row_ref[...]) & earlier
        rank = jnp.sum(same.astype(jnp.int32), axis=0, keepdims=True)
        slot = row_ref[...] * (slots // devices) + rank
        spots = lax.broadcasted_iota(jnp.int32, (slots, rows), 0)
        hot_ref[...] = (spots == slot).astype(jnp.float32).astype(jnp.bfloat16)


def proceed(dists, last, index_ref, doc_ref, q_ref, *refs):
    refs = list(refs)
    blocks = [(d, refs.pop(0), refs.pop(0)) for d in dists]
    old = refs[:3]
    if last:
        hot_ref, out_ref = refs[3:5]
        new = refs[5:]
    else:
        new = refs[3:]
    rows = q_ref.shape[2] // GROUP
    base = index_ref[0] * rows
    earliest = doc_start(doc_ref, base)

    def seen(d):
        return earliest < base - (d - 1) * rows

    def add(d, k_ref, v_ref, source):
        positions = base + lax.broadcasted_iota(jnp.int32, (1, rows), 1)
        visit(d, base, doc_start(doc_ref, positions), positions, q_ref, k_ref, v_ref, source, new)

    def end(source):
        attended = (source[2][0] / source[1][0]).astype(jnp.bfloat16)
        attended = jnp.concatenate([attended[:, g * rows : (g + 1) * rows] for g in range(GROUP)], axis=0)
        out_ref[...] = lax.dot_general(
            hot_ref[...], attended, (((1,), (1,)), ((), ())), preferred_element_type=jnp.float32
        ).astype(jnp.bfloat16)

    @pl.when(seen(dists[0]))
    def _():
        add(*blocks[0], old)
        for block in blocks[1:]:
            pl.when(seen(block[0]))(functools.partial(add, *block, new))
        if last:
            end(new)

    @pl.when(jnp.logical_not(seen(dists[0])))
    def _():
        if last:
            end(old)
        else:
            for source, target in zip(old, new):
                target[...] = source[...]


def join(k_ref, v_ref, out_ref):
    rows = k_ref.shape[0]
    out_ref[:rows] = k_ref[...]
    out_ref[rows:] = v_ref[...]


SMEM = pl.BlockSpec(memory_space=pltpu.SMEM)


def whole(shape):
    return pl.BlockSpec(shape, lambda h: (0,) * len(shape))


def per_head(*shape):
    return pl.BlockSpec((1, *shape), lambda h: (h, 0, 0))


def block_specs(rows):
    return [pl.BlockSpec((rows, HD), lambda h: (0, h)), pl.BlockSpec((rows, HD), lambda h: (1, h))]


def running(rows):
    sizes = [(1, GROUP * rows), (1, GROUP * rows), (HD, GROUP * rows)]
    return [jax.ShapeDtypeStruct((KVH, *s), jnp.float32) for s in sizes], [per_head(*s) for s in sizes]


def cost(rows, blocks):
    return pl.CostEstimate(
        flops=blocks * 4 * rows * rows * H * HD, bytes_accessed=6 << 20, transcendentals=blocks * rows * rows * H
    )


PARAMS = pltpu.CompilerParams(vmem_limit_bytes=32 << 20)


def first_step(index, doc_lengths, queries, block, row_owner, devices):
    rows = block.shape[0] // 2
    shapes, specs = running(rows)
    return pl.pallas_call(
        functools.partial(begin, devices),
        grid=(KVH,),
        in_specs=[
            SMEM, SMEM, pl.BlockSpec((rows, GROUP * HD), lambda h: (0, h)), *block_specs(rows),
            whole((rows, 1)), whole((1, rows)),
        ],
        out_specs=[*specs, per_head(HD, GROUP * rows), whole((2 * rows, rows))],
        out_shape=[
            *shapes,
            jax.ShapeDtypeStruct((KVH, HD, GROUP * rows), jnp.bfloat16),
            jax.ShapeDtypeStruct((2 * rows, rows), jnp.bfloat16),
        ],
        compiler_params=PARAMS,
        cost_estimate=cost(rows, 1),
    )(index, doc_lengths, queries, block, block, row_owner, row_owner.reshape(1, rows))


def next_step(index, doc_lengths, queries, blocks, state):
    rows = blocks[0][1].shape[0] // 2
    shapes, specs = running(rows)
    return pl.pallas_call(
        functools.partial(proceed, [d for d, _ in blocks], False),
        grid=(KVH,),
        in_specs=[SMEM, SMEM, per_head(HD, GROUP * rows), *block_specs(rows) * len(blocks), *specs],
        out_specs=specs,
        out_shape=shapes,
        compiler_params=PARAMS,
        cost_estimate=cost(rows, len(blocks)),
    )(index, doc_lengths, queries, *[b for _, block in blocks for b in (block, block)], *state)


def finish(index_ref, doc_ref, q_ref, k_ref, v_ref, m_ref, l_ref, acc_ref, hot_ref, out_ref, *scratch):
    for h in range(KVH):
        lanes = pl.ds(h * HD, HD)
        proceed(
            [SPAN // 2], True, index_ref, doc_ref, q_ref.at[pl.ds(h, 1)], k_ref.at[:, lanes], v_ref.at[:, lanes],
            *[ref.at[pl.ds(h, 1)] for ref in (m_ref, l_ref, acc_ref)], hot_ref,
            out_ref.at[:, pl.ds(h * GROUP * HD, GROUP * HD)], *scratch,
        )


def last_step(index, doc_lengths, queries, keys, values, state, hot):
    _, specs = running(keys.shape[0])
    vmem = pl.BlockSpec(memory_space=pltpu.VMEM)
    return pl.pallas_call(
        finish,
        in_specs=[SMEM, SMEM] + [vmem] * 7,
        out_specs=vmem,
        out_shape=jax.ShapeDtypeStruct((hot.shape[0], H * HD), jnp.bfloat16),
        scratch_shapes=[pltpu.VMEM(s.block_shape, jnp.float32) for s in specs],
        compiler_params=PARAMS,
        cost_estimate=cost(keys.shape[0], 1),
    )(index, doc_lengths, queries, keys, values, *state, hot)


def joined(keys, values):
    return pl.pallas_call(
        join, out_shape=jax.ShapeDtypeStruct((2 * keys.shape[0], keys.shape[1]), keys.dtype)
    )(keys, values)


def on_device(query_rows, key_rows, value_rows, doc_lengths, row_owner):
    rows, features = query_rows.shape
    devices = lax.axis_size("ctx")
    index = lax.axis_index("ctx").astype(jnp.int32).reshape(1)
    block = joined(key_rows, value_rows)
    near1, far7 = shift(block, 1), shift(block, SPAN - 1)
    *state, queries, hot = first_step(index, doc_lengths, query_rows, block, row_owner, devices)
    near1, *state = lax.optimization_barrier((near1, *state))
    near2, far6 = shift(near1, 1), shift(far7, -1)
    state = next_step(index, doc_lengths, queries, [(1, near1), (7, far7)], state)
    near2, *state = lax.optimization_barrier((near2, *state))
    near3, far5 = shift(near2, 1), shift(far6, -1)
    state = next_step(index, doc_lengths, queries, [(2, near2), (6, far6)], state)
    near3, *state = lax.optimization_barrier((near3, *state))
    k4, v4 = shift(near3[:rows], 1), shift(far5[rows:], -1)
    state = next_step(index, doc_lengths, queries, [(3, near3), (5, far5)], state)
    outgoing = last_step(index, doc_lengths, queries, k4, v4, state, hot)
    received = lax.all_to_all(
        outgoing.reshape(devices, -1, features), "ctx", split_axis=0, concat_axis=0, tiled=True
    )
    return received.reshape(-1, features)


def solution(mesh):
    rows = P(("dp", "ctx"), None)
    return jax.shard_map(
        on_device,
        mesh=mesh,
        in_specs=(rows, rows, rows, P("dp"), rows),
        out_specs=rows,
        check_vma=False,
    )
```
